256 devices in a mesh: section: 16 (over y, z_lo), tensor: 16 (over z_hi, x, core).
Axes of the slice: x: 4, y: 4, z: 8 (z_hi: 2, z_lo: 4; z = z_hi * 4 + z_lo), core: 2. Of those that a mesh axis runs over, the one named last changes fastest.
Arguments:
- heads_out: bfloat16 [16, 1024, 6144], P('section', None, 'tensor'), may hold values from -6 to 6
- projection: bfloat16 [16, 6144, 6144], P('section', 'tensor'), may hold values from -0.078125 to 0.078125
- incoming: bfloat16 [16, 1024, 6144], P('section', 'tensor'), may hold values from -6 to 6
- parked: bfloat16 [16, 1024, 6144], P('section', None, 'tensor'), may hold values from -0.1875 to 0.1875
Outputs:
- activation: bfloat16 [16, 1024, 6144], P('section', 'tensor')
- heads_gradient: bfloat16 [16, 1024, 6144], P('section', None, 'tensor')
- weight_gradient: bfloat16 [16, 6144, 6144], P('section', 'tensor')
The draws below stay inside these ranges and needn't reach their ends.
All inputs are finite; a program needn't handle non-finite values.
Results may differ from the reference program's by a relative error of at most 0.018.
Values may be sent and summed in bfloat16 or wider, within the bound.
A program may use at most 128 MiB of HBM per device.

```python
import jax
import jax.numpy as jnp
from jax import lax

D = 6144
TOKENS = 1024
HEAD_WIDTH = 6144
SECTIONS = 16
N_TENSOR = 16


def block_levels(key, shape, shards, least, largest):
    level, own = 1.0, jax.random.fold_in(key, 6)
    for position, blocks in shards:
        steps = jnp.exp(jax.random.uniform(jax.random.fold_in(own, position), (blocks,), jnp.float32, least / len(shards), largest / len(shards)))
        level = level * jnp.repeat(steps, shape[position] // blocks).reshape([-1 if axis == position else 1 for axis in range(len(shape))])
    return level


def scatter_about(key, extent, width, most, shards=(), kind=jnp.bfloat16):
    factor_of = block_levels(key, extent, shards, -0.22, 0.18) if shards else 1.0
    drawn = jax.random.normal(key, extent, jnp.float32) * width * factor_of
    return jnp.minimum(jnp.maximum(drawn, -most), most).astype(kind)


def setup_inputs(seed: int = 0) -> dict:
    splits = jax.random.split(jax.random.key(seed), 5)
    return {
        "heads_out": scatter_about(splits[0], (SECTIONS, TOKENS, HEAD_WIDTH), 1.0, 6.0, ((0, 16), (2, 16))),
        "projection": scatter_about(splits[1], (SECTIONS, HEAD_WIDTH, D), HEAD_WIDTH ** -0.5, 0.078125, ((0, 16), (1, 16))),
        "incoming": scatter_about(splits[2], (SECTIONS, TOKENS, D), 1.0, 6.0, ((0, 16), (1, 16))),
        "parked": scatter_about(splits[3], (SECTIONS, TOKENS, HEAD_WIDTH), TOKENS ** -0.5, 0.1875, ((0, 16), (2, 16))),
    }


feature_axes = (((1,), (1,)), ((), ()))
token_axes = (((0,), (0,)), ((), ()))


def project_section(paired):
    heads_out, weight = paired
    group_width = weight.shape[0] // N_TENSOR

    def add_group(group, totals):
        offset = (group * group_width).astype(jnp.int32)
        columns = lax.dynamic_slice_in_dim(heads_out, offset, group_width, 1)
        weight_rows = lax.dynamic_slice_in_dim(weight, offset, group_width, 0)
        partial_value = jnp.dot(columns, weight_rows, preferred_element_type=jnp.float32).astype(jnp.bfloat16)
        partial_value = lax.optimization_barrier(partial_value)
        return totals + partial_value.astype(jnp.float32)

    initial = jnp.zeros((heads_out.shape[0], weight.shape[1]), jnp.float32)
    totals = lax.fori_loop(0, N_TENSOR, add_group, initial)
    return totals.astype(jnp.bfloat16)


def backward_section(triple):
    upstream, weight, stored = triple
    heads_grad = lax.dot_general(upstream, weight, feature_axes, preferred_element_type=jnp.float32)
    weight_grad = lax.dot_general(stored, upstream, token_axes, preferred_element_type=jnp.float32)
    return heads_grad.astype(jnp.bfloat16), weight_grad.astype(jnp.bfloat16)


def reference(heads_out, projection, incoming, parked):
    sections = projection.shape[0]
    produced = lax.map(project_section, (heads_out, projection))
    activation = jnp.roll(produced, 1, axis=0)
    upstream = jnp.roll(incoming, -1, axis=0)
    stored = jnp.roll(parked, -(sections // 2), axis=0)
    heads_gradient, weight_gradient = lax.map(backward_section, (upstream, projection, stored))
    return (activation, heads_gradient, weight_gradient)
```

```python
import functools

import jax
import jax.numpy as jnp
from jax import lax
from jax.experimental import pallas as pl
from jax.experimental.pallas import tpu as pltpu
from jax.sharding import PartitionSpec as P

MESH = pl.DeviceIdType.MESH
CHUNKS = 12
ROWS = 64
STAGES = {
    "share": 0,
    "combine": 1,
    "relay": 3,
    "reduce": 5,
    "spread": 7,
    "forward": 9,
    "pair": 11,
    "multiply": 12,
    "finish": 13,
}
TURN_AT = 8
feature_axes = (((1,), (1,)), ((), ()))


def matmul(a, b):
    return jnp.dot(a, b, preferred_element_type=jnp.float32)


def wait_bytes(ref, sem):
    pltpu.make_async_copy(ref, ref, sem).wait()


def kernel(
    heads, weight, incoming, parked,
    activation, heads_gradient, weight_gradient,
    heads_v, weight_v, stored_v, turned_v, up_v, half_v, half_in, sums, relay_in, direct_in, final_in,
    total, heads_out_v, weight_out_v, act_v,
    load_sem, weight_sem, out_sem, send_sem, near_sem, far_sem, left_sem, right_sem, rest_sem, pair_sem,
    share_sem, relay_sem, direct_sem, final_sem, stored_sem,
):
    width = weight_v.shape[2]
    half = heads_v.shape[1]
    section, tensor = lax.axis_index("section"), lax.axis_index("tensor")
    z_lo, z_hi, x, core = section % 4, tensor // 8, (tensor // 2) % 4, tensor % 2
    z = z_hi * 4 + z_lo
    right, left, across = (x + 1) % 4, (x + 3) % 4, (x + 2) % 4
    above, below = (section + 1) % 16, (section + 15) % 16
    up_hi, down_hi = ((z + 1) % 8) // 4, ((z + 7) % 8) // 4

    def member(hi, column):
        return hi * 8 + column * 2 + core

    sibling = (section, tensor + 1 - 2 * core)
    to_right, to_left = (section, member(z_hi, right)), (section, member(z_hi, left))
    near_up, far_up = (above, member(up_hi, x)), (above, member(1 - up_hi, x))
    near_down, far_down = (below, member(down_hi, x)), (below, member(1 - down_hi, x))
    opposite = ((section + 8) % 16, tensor)

    def rows_of(hi, column):
        return pl.ds(pl.multiple_of(core * half + (hi * 4 + column) * ROWS, ROWS), ROWS)

    def own_half():
        return pl.ds(pl.multiple_of(core * half, half), half)

    def send(src, dst, stage, recv, device):
        pltpu.make_async_remote_copy(
            src_ref=src, dst_ref=dst, send_sem=send_sem.at[stage], recv_sem=recv, device_id=device, device_id_type=MESH
        ).start()

    def columns(j):
        return pl.ds(pl.multiple_of(j * width, width), width)

    def load_heads(slot, colour):
        return pltpu.make_async_copy(heads.at[:, colour], heads_v.at[slot].reshape(8, ROWS, heads_v.shape[2]), load_sem.at[slot])

    def load_weight(j):
        return pltpu.make_async_copy(weight.at[:, columns(j)], weight_v.at[j], weight_sem.at[j])

    load_heads(1, 1 - core).start()
    load_weight(0).start()
    load_heads(0, core).start()

    @pl.loop(1, CHUNKS)
    def _(j):
        load_weight(j).start()

    barrier = pltpu.get_barrier_semaphore()
    peers = (sibling, to_right, to_left, near_up, far_up, near_down, far_down, opposite)
    for peer in peers:
        pl.semaphore_signal(barrier, inc=1, device_id=peer, device_id_type=MESH)
    pl.semaphore_wait(barrier, len(peers))

    @pl.loop(0, CHUNKS)
    def _(j):
        own = rows_of(z_hi, x)
        send(incoming.at[:, columns(j)], up_v.at[j, own], 0, far_sem.at[j], far_down)
        send(incoming.at[:, columns(j)], up_v.at[j, own], 0, near_sem.at[j], near_down)

    for colour in range(2):
        send(parked.at[:, colour], stored_v.at[colour], 8, stored_sem, opposite)

    load_heads(1, 1 - core).wait()
    load_heads(0, core).wait()

    def share(j):
        load_weight(j).wait()
        half_v[j] = matmul(heads_v[1], weight_v[j]).astype(jnp.bfloat16)
        send(half_v.at[j], half_in.at[j], 1, share_sem.at[j], sibling)

    def combine(j):
        wait_bytes(half_in.at[j], share_sem.at[j])
        both = matmul(heads_v[0], weight_v[j]) + half_in[j].astype(jnp.float32)
        sums[j] = both.astype(jnp.bfloat16).reshape(2, 4, ROWS, width)
        send(sums.at[j, 0, across], relay_in.at[j, 0], 2, relay_sem.at[j, 0], to_right)
        send(sums.at[j, 1, across], relay_in.at[j, 1], 2, relay_sem.at[j, 1], to_left)
        send(sums.at[j, 1, right], direct_in.at[j, 0, 1], 2, direct_sem.at[j], to_right)
        send(sums.at[j, 0, left], direct_in.at[j, 1, 0], 2, direct_sem.at[j], to_left)

    def relay(j):
        for hi, column, device in ((0, right, to_right), (1, left, to_left)):
            wait_bytes(relay_in.at[j, hi], relay_sem.at[j, hi])
            added = sums[j, hi, column].astype(jnp.float32) + relay_in[j, hi].astype(jnp.float32)
            sums[j, hi, column] = added.astype(jnp.bfloat16)
            send(sums.at[j, hi, column], direct_in.at[j, hi, hi], 3, direct_sem.at[j], device)

    def reduce(j):
        wait_bytes(direct_in.at[j], direct_sem.at[j])
        for hi in range(2):
            added = sums[j, hi, x].astype(jnp.float32) + direct_in[j, 0, hi].astype(jnp.float32)
            sums[j, hi, x] = (added + direct_in[j, 1, hi].astype(jnp.float32)).astype(jnp.bfloat16)
        send(sums.at[j, 1 - up_hi, x], final_in.at[j, 1], 4, final_sem.at[j], far_up)
        send(sums.at[j, up_hi, x], final_in.at[j, 0], 4, final_sem.at[j], near_up)

    def finish(j):
        wait_bytes(final_in.at[j], final_sem.at[j])
        act_v[j] = (final_in[j, 0].astype(jnp.float32) + final_in[j, 1].astype(jnp.float32)).astype(jnp.bfloat16)
        pltpu.make_async_copy(act_v.at[j], activation.at[:, columns(j)], out_sem.at[0]).start()

    def spread(j):
        near, far = up_v.at[j, rows_of(up_hi, x)], up_v.at[j, rows_of(1 - up_hi, x)]
        wait_bytes(near, near_sem.at[j])
        send(near, near, 5, left_sem.at[j], to_right)
        send(near, near, 5, rest_sem.at[j], to_left)
        wait_bytes(far, far_sem.at[j])
        send(far, far, 5, right_sem.at[j], to_left)
        send(far, far, 5, rest_sem.at[j], to_right)

    def forward(j):
        near, far = up_v.at[j, rows_of(up_hi, left)], up_v.at[j, rows_of(1 - up_hi, right)]
        wait_bytes(near, left_sem.at[j])
        send(near, near, 6, rest_sem.at[j], to_right)
        wait_bytes(far, right_sem.at[j])
        send(far, far, 6, rest_sem.at[j], to_left)

    def pair(j):
        wait_bytes(up_v.at[j, pl.ds(0, 4 * ROWS)], rest_sem.at[j])
        mine = up_v.at[j, own_half()]
        send(mine, mine, 7, pair_sem.at[j], sibling)

    def turn():
        wait_bytes(stored_v, stored_sem)
        turned_v[...] = stored_v[...].reshape(2 * half, stored_v.shape[3]).T

    def multiply(j):
        wait_bytes(up_v.at[j, pl.ds(0, half)], pair_sem.at[j])
        block = up_v[j]
        term = lax.dot_general(block, weight_v[j], feature_axes, preferred_element_type=jnp.float32)

        @pl.when(j == 0)
        def _():
            total[...] = term

        @pl.when(j > 0)
        def _():
            total[...] += term

        @pl.when(j == CHUNKS - 1)
        def _():
            heads_out_v[...] = total[...].astype(jnp.bfloat16).reshape(heads_out_v.shape)
            for colour in range(2):
                pltpu.make_async_copy(heads_out_v.at[colour], heads_gradient.at[:, colour], out_sem.at[1]).start()

        weight_out_v[j] = matmul(turned_v[...], block).astype(jnp.bfloat16)
        pltpu.make_async_copy(weight_out_v.at[j], weight_gradient.at[:, columns(j)], out_sem.at[2]).start()

    stages = dict(
        share=share, combine=combine, relay=relay, reduce=reduce, spread=spread, forward=forward, pair=pair,
        multiply=multiply, finish=finish,
    )

    @pl.loop(0, CHUNKS + max(STAGES.values()))
    def _(i):
        for name, start in STAGES.items():
            pl.when((i >= start) & (i < start + CHUNKS))(functools.partial(stages[name], i - start))
        pl.when(i == TURN_AT)(turn)

    for stage, ref in ((0, final_in), (1, half_v), (2, direct_in), (3, final_in), (4, final_in), (5, direct_in), (6, final_in), (7, half_v), (8, stored_v)):
        wait_bytes(ref, send_sem.at[stage])
    wait_bytes(act_v, out_sem.at[0])
    wait_bytes(heads_out_v, out_sem.at[1])
    wait_bytes(weight_out_v, out_sem.at[2])


def section_step(heads_out, projection, incoming, parked):
    weight = projection[0]
    depth, model = weight.shape
    tokens = heads_out.shape[1]
    half, width = tokens // 2, model // CHUNKS
    blocked = (8, 2, ROWS, depth)
    bf16, f32 = jnp.bfloat16, jnp.float32
    dma = pltpu.SemaphoreType.DMA
    per_chunk = dma((CHUNKS,))
    outs = pl.pallas_call(
        kernel,
        out_shape=(
            jax.ShapeDtypeStruct((ROWS, model), bf16),
            jax.ShapeDtypeStruct(blocked, bf16),
            jax.ShapeDtypeStruct((depth, model), bf16),
        ),
        in_specs=[pl.BlockSpec(memory_space=pl.ANY)] * 4,
        out_specs=[pl.BlockSpec(memory_space=pl.ANY)] * 3,
        scratch_shapes=[
            pltpu.VMEM((2, half, depth), bf16),
            pltpu.VMEM((CHUNKS, depth, width), bf16),
            pltpu.VMEM((2, 8, ROWS, depth), bf16),
            pltpu.VMEM((depth, tokens), bf16),
            pltpu.VMEM((CHUNKS, tokens, width), bf16),
            pltpu.VMEM((CHUNKS, half, width), bf16),
            pltpu.VMEM((CHUNKS, half, width), bf16),
            pltpu.VMEM((CHUNKS, 2, 4, ROWS, width), bf16),
            pltpu.VMEM((CHUNKS, 2, ROWS, width), bf16),
            pltpu.VMEM((CHUNKS, 2, 2, ROWS, width), bf16),
            pltpu.VMEM((CHUNKS, 2, ROWS, width), bf16),
            pltpu.VMEM((tokens, depth), f32),
            pltpu.VMEM((2, 8, ROWS, depth), bf16),
            pltpu.VMEM((CHUNKS, depth, width), bf16),
            pltpu.VMEM((CHUNKS, ROWS, width), bf16),
            dma((2,)),
            per_chunk,
            dma((3,)),
            dma((9,)),
            per_chunk,
            per_chunk,
            per_chunk,
            per_chunk,
            per_chunk,
            per_chunk,
            per_chunk,
            dma((CHUNKS, 2)),
            per_chunk,
            per_chunk,
            dma,
        ],
        compiler_params=pltpu.CompilerParams(collective_id=0, has_side_effects=True, vmem_limit_bytes=62 << 20),
        cost_estimate=pl.CostEstimate(flops=6 * tokens * depth * model, bytes_accessed=14 << 20, transcendentals=0),
        name="relay_section",
    )(heads_out.reshape(blocked), weight, incoming[0], parked.reshape(blocked))
    activation, heads_gradient, weight_gradient = outs
    return activation[None], heads_gradient.reshape(1, tokens, depth), weight_gradient[None]


def solution(mesh):
    whole_tokens = P("section", None, "tensor")
    rows = P("section", "tensor", None)
    return jax.shard_map(
        section_step,
        mesh=mesh,
        in_specs=(whole_tokens, rows, rows, whole_tokens),
        out_specs=(rows, whole_tokens, rows),
        check_vma=False,
    )
```

```python
import functools

import jax
import jax.numpy as jnp
from jax import lax
from jax.experimental import pallas as pl
from jax.experimental.pallas import tpu as pltpu
from jax.sharding import PartitionSpec as P

MESH = pl.DeviceIdType.MESH
CHUNKS = 12
ROWS = 64
STAGES = {
    "share": 0,
    "combine": 1,
    "relay": 3,
    "reduce": 6,
    "spread": 3,
    "forward": 6,
    "pair": 9,
    "multiply": 10,
    "finish": 12,
}
CROSSED = 2
CROSS = {"cross": 9, "pair": 13, "multiply": 14}
FETCH_AT = 1
TURN_AT = 9
feature_axes = (((1,), (1,)), ((), ()))


def matmul(a, b):
    return jnp.dot(a, b, preferred_element_type=jnp.float32)


def wait_bytes(ref, sem):
    pltpu.make_async_copy(ref, ref, sem).wait()


def kernel(
    heads, weight, incoming, parked,
    act_v, heads_out_v, weight_out_v,
    heads_v, weight_v, stored_v, turned_v, up_v, half_v, half_in, sums, relay_in, direct_in, final_in,
    total,
    load_sem, weight_sem, send_sem, near_sem, far_sem, left_sem, right_sem, rest_sem, pair_sem,
    share_sem, relay_sem, direct_sem, final_sem, stored_sem, cross_sem,
):
    width = weight_v.shape[2]
    half = heads_v.shape[1]
    section, tensor = lax.axis_index("section"), lax.axis_index("tensor")
    z_lo, z_hi, x, core = section % 4, tensor // 8, (tensor // 2) % 4, tensor % 2
    z = z_hi * 4 + z_lo
    right, left, across = (x + 1) % 4, (x + 3) % 4, (x + 2) % 4
    above, below = (section + 1) % 16, (section + 15) % 16
    up_hi, down_hi = ((z + 1) % 8) // 4, ((z + 7) % 8) // 4

    def member(hi, column):
        return hi * 8 + column * 2 + core

    sibling = (section, tensor + 1 - 2 * core)
    to_right, to_left = (section, member(z_hi, right)), (section, member(z_hi, left))
    near_up, far_up = (above, member(up_hi, x)), (above, member(1 - up_hi, x))
    near_down, far_down = (below, member(down_hi, x)), (below, member(1 - down_hi, x))
    opposite, partner = ((section + 8) % 16, tensor), (section, (tensor + 8) % 16)

    def rows_of(hi, column):
        return pl.ds(pl.multiple_of(core * half + (hi * 4 + column) * ROWS, ROWS), ROWS)

    def own_half():
        return pl.ds(pl.multiple_of(core * half, half), half)

    def send(src, dst, stage, recv, device):
        pltpu.make_async_remote_copy(
            src_ref=src, dst_ref=dst, send_sem=send_sem.at[stage], recv_sem=recv, device_id=device, device_id_type=MESH
        ).start()

    def columns(j):
        return pl.ds(pl.multiple_of(j * width, width), width)

    def load_heads(slot, colour):
        return pltpu.make_async_copy(heads.at[:, colour], heads_v.at[slot].reshape(8, ROWS, heads_v.shape[2]), load_sem.at[slot])

    def load_weight(j):
        return pltpu.make_async_copy(weight.at[:, columns(j)], weight_v.at[j], weight_sem.at[j])

    load_heads(1, 1 - core).start()
    load_weight(0).start()
    load_heads(0, core).start()

    @pl.loop(1, CHUNKS)
    def _(j):
        load_weight(j).start()

    barrier = pltpu.get_barrier_semaphore()
    peers = (sibling, to_right, to_left, near_up, far_up, near_down, far_down, opposite, partner)
    for peer in peers:
        pl.semaphore_signal(barrier, inc=1, device_id=peer, device_id_type=MESH)
    pl.semaphore_wait(barrier, len(peers))

    @pl.loop(0, CHUNKS)
    def _(j):
        own = rows_of(z_hi, x)
        send(incoming.at[:, columns(j)], up_v.at[j, own], 0, near_sem.at[j], near_down)

        @pl.when(j >= CROSSED)
        def _():
            send(incoming.at[:, columns(j)], up_v.at[j, own], 0, far_sem.at[j], far_down)

    load_heads(1, 1 - core).wait()
    load_heads(0, core).wait()

    def share(j):
        load_weight(j).wait()
        half_v[j] = matmul(heads_v[1], weight_v[j]).astype(jnp.bfloat16)
        send(half_v.at[j], half_in.at[j], 1, share_sem.at[j], sibling)

    def combine(j):
        wait_bytes(half_in.at[j], share_sem.at[j])
        both = matmul(heads_v[0], weight_v[j]) + half_in[j].astype(jnp.float32)
        sums[j] = both.astype(jnp.bfloat16).reshape(2, 4, ROWS, width)
        send(sums.at[j, 0, across], relay_in.at[j, 0], 2, relay_sem.at[j, 0], to_right)
        send(sums.at[j, 1, across], relay_in.at[j, 1], 2, relay_sem.at[j, 1], to_left)
        send(sums.at[j, 1, right], direct_in.at[j, 0, 1], 2, direct_sem.at[j], to_right)
        send(sums.at[j, 0, left], direct_in.at[j, 1, 0], 2, direct_sem.at[j], to_left)

    def relay(j):
        for hi, column, device in ((0, right, to_right), (1, left, to_left)):
            wait_bytes(relay_in.at[j, hi], relay_sem.at[j, hi])
            added = sums[j, hi, column].astype(jnp.float32) + relay_in[j, hi].astype(jnp.float32)
            sums[j, hi, column] = added.astype(jnp.bfloat16)
            send(sums.at[j, hi, column], direct_in.at[j, hi, hi], 3, direct_sem.at[j], device)

    def reduce(j):
        wait_bytes(direct_in.at[j], direct_sem.at[j])
        for hi in range(2):
            added = sums[j, hi, x].astype(jnp.float32) + direct_in[j, 0, hi].astype(jnp.float32)
            sums[j, hi, x] = (added + direct_in[j, 1, hi].astype(jnp.float32)).astype(jnp.bfloat16)
        send(sums.at[j, 1 - up_hi, x], final_in.at[j, 1], 4, final_sem.at[j], far_up)
        send(sums.at[j, up_hi, x], final_in.at[j, 0], 4, final_sem.at[j], near_up)

    def finish(j):
        wait_bytes(final_in.at[j], final_sem.at[j])
        act_v[j] = (final_in[j, 0].astype(jnp.float32) + final_in[j, 1].astype(jnp.float32)).astype(jnp.bfloat16)

    def spread(j):
        near, far = up_v.at[j, rows_of(up_hi, x)], up_v.at[j, rows_of(1 - up_hi, x)]
        wait_bytes(near, near_sem.at[j])
        send(near, near, 5, left_sem.at[j], to_right)
        send(near, near, 5, rest_sem.at[j], to_left)

        @pl.when(j >= CROSSED)
        def _():
            wait_bytes(far, far_sem.at[j])
            send(far, far, 5, right_sem.at[j], to_left)
            send(far, far, 5, rest_sem.at[j], to_right)

    def forward(j):
        near, far = up_v.at[j, rows_of(up_hi, left)], up_v.at[j, rows_of(1 - up_hi, right)]
        wait_bytes(near, left_sem.at[j])
        send(near, near, 6, rest_sem.at[j], to_right)

        @pl.when(j >= CROSSED)
        def _():
            wait_bytes(far, right_sem.at[j])
            send(far, far, 6, rest_sem.at[j], to_left)

    def cross(j):
        wait_bytes(up_v.at[j, pl.ds(0, 2 * ROWS)], rest_sem.at[j])
        mine = up_v.at[j, pl.ds(pl.multiple_of(core * half + up_hi * 4 * ROWS, 4 * ROWS), 4 * ROWS)]
        send(mine, mine, 9, cross_sem.at[j], partner)

    def pair(j):
        @pl.when(j >= CROSSED)
        def _():
            wait_bytes(up_v.at[j, pl.ds(0, 4 * ROWS)], rest_sem.at[j])

        @pl.when(j < CROSSED)
        def _():
            wait_bytes(up_v.at[j, pl.ds(0, 4 * ROWS)], cross_sem.at[j])

        mine = up_v.at[j, own_half()]
        send(mine, mine, 7, pair_sem.at[j], sibling)

    def fetch_stored(block):
        for colour in range(2):
            send(parked.at[block, colour], stored_v.at[colour, block], 8, stored_sem, opposite)

    def turn():
        wait_bytes(stored_v, stored_sem)
        turned_v[...] = stored_v[...].reshape(2 * half, stored_v.shape[3]).T

    def multiply(j):
        wait_bytes(up_v.at[j, pl.ds(0, half)], pair_sem.at[j])
        block = up_v[j]
        term = lax.dot_general(block, weight_v[j], feature_axes, preferred_element_type=jnp.float32)

        total[...] += term
        weight_out_v[j] = matmul(turned_v[...], block).astype(jnp.bfloat16)

    stages = dict(
        share=share, combine=combine, relay=relay, reduce=reduce, spread=spread, forward=forward, pair=pair,
        multiply=multiply, finish=finish, cross=cross,
    )

    total[...] = jnp.zeros_like(total)

    @pl.loop(0, CHUNKS + max(STAGES.values()))
    def _(i):
        pl.when((i >= FETCH_AT) & (i < FETCH_AT + 8))(lambda: fetch_stored(i - FETCH_AT))
        pl.when(i == TURN_AT)(turn)
        for name, start in STAGES.items():
            first = CROSSED if name in CROSS else 0
            pl.when((i >= start + first) & (i < start + CHUNKS))(functools.partial(stages[name], i - start))
        for name, start in CROSS.items():
            pl.when((i >= start) & (i < start + CROSSED))(functools.partial(stages[name], i - start))

    heads_out_v[...] = total[...].astype(jnp.bfloat16).reshape(heads_out_v.shape)
    blocks = half_v.reshape(CHUNKS * 8, ROWS, width)
    sent = {
        0: 2 * CHUNKS - CROSSED,
        1: 8 * CHUNKS,
        2: 4 * CHUNKS,
        3: 2 * CHUNKS,
        4: 2 * CHUNKS,
        5: 4 * CHUNKS - 2 * CROSSED,
        6: 2 * CHUNKS - CROSSED,
        7: 8 * CHUNKS,
        9: 4 * CROSSED,
    }
    for stage, count in sent.items():
        wait_bytes(blocks.at[pl.ds(0, count)], send_sem.at[stage])
    wait_bytes(stored_v, send_sem.at[8])


def publish(act_v, heads_out_v, weight_out_v, activation, heads_gradient, weight_gradient, sem):
    width = act_v.shape[2]
    copies = [pltpu.make_async_copy(heads_out_v.at[colour], heads_gradient.at[:, colour], sem.at[0]) for colour in range(2)]
    for j in range(CHUNKS):
        columns = pl.ds(j * width, width)
        copies.append(pltpu.make_async_copy(weight_out_v.at[j], weight_gradient.at[:, columns], sem.at[1]))
        copies.append(pltpu.make_async_copy(act_v.at[j], activation.at[:, columns], sem.at[2]))
    for copy in copies:
        copy.start()
    wait_bytes(heads_out_v, sem.at[0])
    wait_bytes(weight_out_v, sem.at[1])
    wait_bytes(act_v, sem.at[2])


def section_step(heads_out, projection, incoming, parked):
    weight = projection[0]
    depth, model = weight.shape
    tokens = heads_out.shape[1]
    half, width = tokens // 2, model // CHUNKS
    blocked = (8, 2, ROWS, depth)
    bf16, f32 = jnp.bfloat16, jnp.float32
    dma = pltpu.SemaphoreType.DMA
    per_chunk = dma((CHUNKS,))
    outs = pl.pallas_call(
        kernel,
        out_shape=(
            pltpu.VMEM((CHUNKS, ROWS, width), bf16),
            pltpu.VMEM((2, 8, ROWS, depth), bf16),
            pltpu.VMEM((CHUNKS, depth, width), bf16),
        ),
        in_specs=[pl.BlockSpec(memory_space=pl.ANY)] * 4,
        out_specs=[pl.BlockSpec(memory_space=pltpu.VMEM)] * 3,
        scratch_shapes=[
            pltpu.VMEM((2, half, depth), bf16),
            pltpu.VMEM((CHUNKS, depth, width), bf16),
            pltpu.VMEM((2, 8, ROWS, depth), bf16),
            pltpu.VMEM((depth, tokens), bf16),
            pltpu.VMEM((CHUNKS, tokens, width), bf16),
            pltpu.VMEM((CHUNKS, half, width), bf16),
            pltpu.VMEM((CHUNKS, half, width), bf16),
            pltpu.VMEM((CHUNKS, 2, 4, ROWS, width), bf16),
            pltpu.VMEM((CHUNKS, 2, ROWS, width), bf16),
            pltpu.VMEM((CHUNKS, 2, 2, ROWS, width), bf16),
            pltpu.VMEM((CHUNKS, 2, ROWS, width), bf16),
            pltpu.VMEM((tokens, depth), f32),
            dma((2,)),
            per_chunk,
            dma((10,)),
            per_chunk,
            per_chunk,
            per_chunk,
            per_chunk,
            per_chunk,
            per_chunk,
            per_chunk,
            dma((CHUNKS, 2)),
            per_chunk,
            per_chunk,
            dma,
            per_chunk,
        ],
        compiler_params=pltpu.CompilerParams(collective_id=0, has_side_effects=True, vmem_limit_bytes=52 << 20),
        cost_estimate=pl.CostEstimate(flops=6 * tokens * depth * model, bytes_accessed=14 << 20, transcendentals=0),
        name="relay_section",
    )(heads_out.reshape(blocked), weight, incoming[0], parked.reshape(blocked))
    activation, heads_gradient, weight_gradient = pl.pallas_call(
        publish,
        out_shape=(
            jax.ShapeDtypeStruct((ROWS, model), bf16),
            jax.ShapeDtypeStruct(blocked, bf16),
            jax.ShapeDtypeStruct((depth, model), bf16),
        ),
        in_specs=[pl.BlockSpec(memory_space=pltpu.VMEM)] * 3,
        out_specs=[pl.BlockSpec(memory_space=pl.ANY)] * 3,
        scratch_shapes=[dma((3,))],
        compiler_params=pltpu.CompilerParams(vmem_limit_bytes=2 << 20),
        name="publish",
    )(*(pltpu.with_memory_space_constraint(out, pltpu.VMEM) for out in outs))
    return activation[None], heads_gradient.reshape(1, tokens, depth), weight_gradient[None]


def solution(mesh):
    whole_tokens = P("section", None, "tensor")
    rows = P("section", "tensor", None)
    return jax.shard_map(
        section_step,
        mesh=mesh,
        in_specs=(whole_tokens, rows, rows, whole_tokens),
        out_specs=(rows, whole_tokens, rows),
        check_vma=False,
    )
```

```python
import functools

import jax
import jax.numpy as jnp
from jax import lax
from jax.experimental import pallas as pl
from jax.experimental.pallas import tpu as pltpu
from jax.sharding import PartitionSpec as P

MESH = pl.DeviceIdType.MESH
CHUNKS = 12
ROWS = 64
STAGES = {
    "launch": -4,
    "share": -1,
    "combine": 0,
    "relay": 2,
    "reduce": 4,
    "spread": 2,
    "forward": 4,
    "pair": 6,
    "multiply": 7,
    "finish": 9,
}
CROSSED = 2
CROSS = {"spread": -1, "cross": 7, "pair": 11, "multiply": 12}
FETCH_AT = 1
TURN_AT = 8
feature_axes = (((1,), (1,)), ((), ()))


def matmul(a, b):
    return jnp.dot(a, b, preferred_element_type=jnp.float32)


def wait_bytes(ref, sem):
    pltpu.make_async_copy(ref, ref, sem).wait()


def kernel(
    heads, weight, incoming, parked,
    act_v, total, turned_v, weight_out_v, block_v, last_weight_v,
    heads_v, weight_v, stored_v, up_v, half_v, half_in, sums, relay_in, direct_in, final_in,
    load_sem, weight_sem, send_sem, near_sem, far_sem, left_sem, right_sem, rest_sem, pair_sem,
    share_sem, relay_sem, direct_sem, final_sem, stored_sem, cross_sem,
):
    width = weight_v.shape[2]
    half = heads_v.shape[1]
    section, tensor = lax.axis_index("section"), lax.axis_index("tensor")
    z_lo, z_hi, x, core = section % 4, tensor // 8, (tensor // 2) % 4, tensor % 2
    z = z_hi * 4 + z_lo
    right, left, across = (x + 1) % 4, (x + 3) % 4, (x + 2) % 4
    above, below = (section + 1) % 16, (section + 15) % 16
    up_hi, down_hi = ((z + 1) % 8) // 4, ((z + 7) % 8) // 4

    def member(hi, column):
        return hi * 8 + column * 2 + core

    sibling = (section, tensor + 1 - 2 * core)
    to_right, to_left = (section, member(z_hi, right)), (section, member(z_hi, left))
    near_up, far_up = (above, member(up_hi, x)), (above, member(1 - up_hi, x))
    near_down, far_down = (below, member(down_hi, x)), (below, member(1 - down_hi, x))
    opposite, partner = ((section + 8) % 16, tensor), (section, (tensor + 8) % 16)

    def rows_of(hi, column):
        return pl.ds(pl.multiple_of(core * half + (hi * 4 + column) * ROWS, ROWS), ROWS)

    def own_half():
        return pl.ds(pl.multiple_of(core * half, half), half)

    def send(src, dst, stage, recv, device):
        pltpu.make_async_remote_copy(
            src_ref=src, dst_ref=dst, send_sem=send_sem.at[stage], recv_sem=recv, device_id=device, device_id_type=MESH
        ).start()

    def columns(j):
        return pl.ds(pl.multiple_of(j * width, width), width)

    def load_heads(slot, colour):
        return pltpu.make_async_copy(heads.at[:, colour], heads_v.at[slot].reshape(8, ROWS, heads_v.shape[2]), load_sem.at[slot])

    def load_weight(j):
        return pltpu.make_async_copy(weight.at[:, columns(j)], weight_v.at[j], weight_sem.at[j])

    load_heads(1, 1 - core).start()
    load_weight(0).start()
    load_heads(0, core).start()

    @pl.loop(1, CHUNKS)
    def _(j):
        load_weight(j).start()

    barrier = pltpu.get_barrier_semaphore()
    peers = (sibling, to_right, to_left, near_up, far_up, near_down, far_down, opposite, partner)
    for peer in peers:
        pl.semaphore_signal(barrier, inc=1, device_id=peer, device_id_type=MESH)

    def project(j):
        load_weight(j).wait()
        half_v[j] = matmul(heads_v[1], weight_v[j]).astype(jnp.bfloat16)

    def send_half(j):
        send(half_v.at[j], half_in.at[j], 1, share_sem.at[j], sibling)

    def share(j):
        project(j)
        send_half(j)

    def launch(j):
        own = rows_of(z_hi, x)
        send(incoming.at[:, columns(j)], up_v.at[j, own], 0, near_sem.at[j], near_down)

        @pl.when(j >= CROSSED)
        def _():
            send(incoming.at[:, columns(j)], up_v.at[j, own], 0, far_sem.at[j], far_down)

    def combine(j):
        wait_bytes(half_in.at[j], share_sem.at[j])
        both = matmul(heads_v[0], weight_v[j]) + half_in[j].astype(jnp.float32)
        sums[j] = both.astype(jnp.bfloat16).reshape(2, 4, ROWS, width)
        send(sums.at[j, 0, across], relay_in.at[j, 0], 2, relay_sem.at[j, 0], to_right)
        send(sums.at[j, 1, across], relay_in.at[j, 1], 2, relay_sem.at[j, 1], to_left)
        send(sums.at[j, 1, right], direct_in.at[j, 0, 1], 2, direct_sem.at[j], to_right)
        send(sums.at[j, 0, left], direct_in.at[j, 1, 0], 2, direct_sem.at[j], to_left)

    def relay(j):
        for hi, column, device in ((0, right, to_right), (1, left, to_left)):
            wait_bytes(relay_in.at[j, hi], relay_sem.at[j, hi])
            added = sums[j, hi, column].astype(jnp.float32) + relay_in[j, hi].astype(jnp.float32)
            sums[j, hi, column] = added.astype(jnp.bfloat16)
            send(sums.at[j, hi, column], direct_in.at[j, hi, hi], 3, direct_sem.at[j], device)

    def reduce(j):
        wait_bytes(direct_in.at[j], direct_sem.at[j])
        for hi in range(2):
            added = sums[j, hi, x].astype(jnp.float32) + direct_in[j, 0, hi].astype(jnp.float32)
            sums[j, hi, x] = (added + direct_in[j, 1, hi].astype(jnp.float32)).astype(jnp.bfloat16)
        send(sums.at[j, 1 - up_hi, x], final_in.at[j, 1], 4, final_sem.at[j], far_up)
        send(sums.at[j, up_hi, x], final_in.at[j, 0], 4, final_sem.at[j], near_up)

    def finish(j):
        wait_bytes(final_in.at[j], final_sem.at[j])
        act_v[j] = (final_in[j, 0].astype(jnp.float32) + final_in[j, 1].astype(jnp.float32)).astype(jnp.bfloat16)

    def spread(j):
        near, far = up_v.at[j, rows_of(up_hi, x)], up_v.at[j, rows_of(1 - up_hi, x)]
        wait_bytes(near, near_sem.at[j])
        send(near, near, 5, left_sem.at[j], to_right)

        @pl.when(j < CROSSED)
        def _():
            send(near, near, 5, rest_sem.at[j], to_left)

        @pl.when(j >= CROSSED)
        def _():
            wait_bytes(far, far_sem.at[j])
            send(far, far, 5, right_sem.at[j], to_left)

    def forward(j):
        near, far = up_v.at[j, rows_of(up_hi, x)], up_v.at[j, rows_of(1 - up_hi, x)]

        @pl.when(j >= CROSSED)
        def _():
            send(near, near, 5, rest_sem.at[j], to_left)
            send(far, far, 5, rest_sem.at[j], to_right)

        passed_near, passed_far = up_v.at[j, rows_of(up_hi, left)], up_v.at[j, rows_of(1 - up_hi, right)]
        wait_bytes(passed_near, left_sem.at[j])
        send(passed_near, passed_near, 6, rest_sem.at[j], to_right)

        @pl.when(j >= CROSSED)
        def _():
            wait_bytes(passed_far, right_sem.at[j])
            send(passed_far, passed_far, 6, rest_sem.at[j], to_left)

    def cross(j):
        wait_bytes(up_v.at[j, pl.ds(0, 2 * ROWS)], rest_sem.at[j])
        mine = up_v.at[j, pl.ds(pl.multiple_of(core * half + up_hi * 4 * ROWS, 4 * ROWS), 4 * ROWS)]
        send(mine, mine, 9, cross_sem.at[j], partner)

    def pair(j):
        @pl.when(j >= CROSSED)
        def _():
            wait_bytes(up_v.at[j, pl.ds(0, 4 * ROWS)], rest_sem.at[j])

        @pl.when(j < CROSSED)
        def _():
            wait_bytes(up_v.at[j, pl.ds(0, 4 * ROWS)], cross_sem.at[j])

        mine = up_v.at[j, own_half()]
        send(mine, mine, 7, pair_sem.at[j], sibling)

    def fetch_stored(block):
        for colour in range(2):
            send(parked.at[block, colour], stored_v.at[colour, block], 8, stored_sem, opposite)

    def turn():
        wait_bytes(stored_v, stored_sem)
        turned_v[...] = stored_v[...].reshape(2 * half, stored_v.shape[3]).T

    def multiply(j):
        wait_bytes(up_v.at[j, pl.ds(0, half)], pair_sem.at[j])
        block = up_v[j]
        term = lax.dot_general(block, weight_v[j], feature_axes, preferred_element_type=jnp.float32)

        total[...] += term
        weight_out_v[j] = matmul(turned_v[...], block).astype(jnp.bfloat16)

    stages = dict(
        launch=launch, share=share, combine=combine, relay=relay, reduce=reduce, spread=spread, forward=forward, pair=pair,
        multiply=multiply, finish=finish, cross=cross,
    )

    load_heads(1, 1 - core).wait()
    project(0)
    pl.semaphore_wait(barrier, len(peers))
    send_half(0)
    pl.loop(0, -STAGES["launch"])(launch)
    total[...] = jnp.zeros_like(total)
    load_heads(0, core).wait()
    for j in range(-CROSS["spread"]):
        spread(j)

    @pl.loop(0, CHUNKS + max(STAGES.values()))
    def _(i):
        pl.when((i >= FETCH_AT) & (i < FETCH_AT + 8))(lambda: fetch_stored(i - FETCH_AT))
        pl.when(i == TURN_AT)(turn)
        for name, start in STAGES.items():
            first = CROSSED if name in CROSS else max(-start, 0)
            count = CHUNKS - 1 if name == "multiply" else CHUNKS
            pl.when((i >= start + first) & (i < start + count))(functools.partial(stages[name], i - start))
        for name, start in CROSS.items():
            pl.when((i >= max(start, 0)) & (i < start + CROSSED))(functools.partial(stages[name], i - start))

    wait_bytes(up_v.at[CHUNKS - 1, pl.ds(0, half)], pair_sem.at[CHUNKS - 1])
    block_v[...] = up_v[CHUNKS - 1]
    last_weight_v[...] = weight_v[CHUNKS - 1]
    blocks = half_v.reshape(CHUNKS * 8, ROWS, width)
    sent = {
        0: 2 * CHUNKS - CROSSED,
        1: 8 * CHUNKS,
        2: 4 * CHUNKS,
        3: 2 * CHUNKS,
        4: 2 * CHUNKS,
        5: 4 * CHUNKS - 2 * CROSSED,
        6: 2 * CHUNKS - CROSSED,
        7: 8 * CHUNKS,
        9: 4 * CROSSED,
    }
    for stage, count in sent.items():
        wait_bytes(blocks.at[pl.ds(0, count)], send_sem.at[stage])
    wait_bytes(stored_v, send_sem.at[8])


def publish(
    act_v, total, turned_v, weight_out_v, block_v, last_weight_v,
    activation, heads_gradient, weight_gradient,
    heads_out_v, last_v, sem,
):
    width = act_v.shape[2]

    def columns(j):
        return pl.ds(j * width, width)

    for j in range(CHUNKS - 1):
        pltpu.make_async_copy(weight_out_v.at[j], weight_gradient.at[:, columns(j)], sem.at[0]).start()
    for j in range(CHUNKS):
        pltpu.make_async_copy(act_v.at[j], activation.at[:, columns(j)], sem.at[1]).start()
    block = block_v[...]
    term = lax.dot_general(block, last_weight_v[...], feature_axes, preferred_element_type=jnp.float32)
    heads_out_v[...] = (total[...] + term).astype(jnp.bfloat16).reshape(heads_out_v.shape)
    for colour in range(2):
        pltpu.make_async_copy(heads_out_v.at[colour], heads_gradient.at[:, colour], sem.at[2]).start()
    last_v[...] = matmul(turned_v[...], block).astype(jnp.bfloat16)
    pltpu.make_async_copy(last_v, weight_gradient.at[:, columns(CHUNKS - 1)], sem.at[3]).start()
    wait_bytes(weight_out_v, sem.at[0])
    wait_bytes(act_v, sem.at[1])
    wait_bytes(heads_out_v, sem.at[2])
    wait_bytes(last_v, sem.at[3])


def section_step(heads_out, projection, incoming, parked):
    weight = projection[0]
    depth, model = weight.shape
    tokens = heads_out.shape[1]
    half, width = tokens // 2, model // CHUNKS
    blocked = (8, 2, ROWS, depth)
    bf16, f32 = jnp.bfloat16, jnp.float32
    dma = pltpu.SemaphoreType.DMA
    per_chunk = dma((CHUNKS,))
    outs = pl.pallas_call(
        kernel,
        out_shape=(
            pltpu.VMEM((CHUNKS, ROWS, width), bf16),
            pltpu.VMEM((tokens, depth), f32),
            pltpu.VMEM((depth, tokens), bf16),
            pltpu.VMEM((CHUNKS - 1, depth, width), bf16),
            pltpu.VMEM((tokens, width), bf16),
            pltpu.VMEM((depth, width), bf16),
        ),
        in_specs=[pl.BlockSpec(memory_space=pl.ANY)] * 4,
        out_specs=[pl.BlockSpec(memory_space=pltpu.VMEM)] * 6,
        scratch_shapes=[
            pltpu.VMEM((2, half, depth), bf16),
            pltpu.VMEM((CHUNKS, depth, width), bf16),
            pltpu.VMEM((2, 8, ROWS, depth), bf16),
            pltpu.VMEM((CHUNKS, tokens, width), bf16),
            pltpu.VMEM((CHUNKS, half, width), bf16),
            pltpu.VMEM((CHUNKS, half, width), bf16),
            pltpu.VMEM((CHUNKS, 2, 4, ROWS, width), bf16),
            pltpu.VMEM((CHUNKS, 2, ROWS, width), bf16),
            pltpu.VMEM((CHUNKS, 2, 2, ROWS, width), bf16),
            pltpu.VMEM((CHUNKS, 2, ROWS, width), bf16),
            dma((2,)),
            per_chunk,
            dma((10,)),
            per_chunk,
            per_chunk,
            per_chunk,
            per_chunk,
            per_chunk,
            per_chunk,
            per_chunk,
            dma((CHUNKS, 2)),
            per_chunk,
            per_chunk,
            dma,
            per_chunk,
        ],
        compiler_params=pltpu.CompilerParams(collective_id=0, has_side_effects=True, vmem_limit_bytes=50 << 20),
        cost_estimate=pl.CostEstimate(flops=6 * tokens * depth * model, bytes_accessed=14 << 20, transcendentals=0),
        name="relay_section",
    )(heads_out.reshape(blocked), weight, incoming[0], parked.reshape(blocked))
    activation, heads_gradient, weight_gradient = pl.pallas_call(
        publish,
        out_shape=(
            jax.ShapeDtypeStruct((ROWS, model), bf16),
            jax.ShapeDtypeStruct(blocked, bf16),
            jax.ShapeDtypeStruct((depth, model), bf16),
        ),
        in_specs=[pl.BlockSpec(memory_space=pltpu.VMEM)] * 6,
        out_specs=[pl.BlockSpec(memory_space=pl.ANY)] * 3,
        scratch_shapes=[pltpu.VMEM((2, 8, ROWS, depth), bf16), pltpu.VMEM((depth, width), bf16), dma((4,))],
        compiler_params=pltpu.CompilerParams(vmem_limit_bytes=12 << 20),
        name="publish",
    )(*(pltpu.with_memory_space_constraint(out, pltpu.VMEM) for out in outs))
    return activation[None], heads_gradient.reshape(1, tokens, depth), weight_gradient[None]


def solution(mesh):
    whole_tokens = P("section", None, "tensor")
    rows = P("section", "tensor", None)
    return jax.shard_map(
        section_step,
        mesh=mesh,
        in_specs=(whole_tokens, rows, rows, whole_tokens),
        out_specs=(rows, whole_tokens, rows),
        check_vma=False,
    )
```

```python
import functools

import jax
import jax.numpy as jnp
from jax import lax
from jax.experimental import pallas as pl
from jax.experimental.pallas import tpu as pltpu
from jax.sharding import PartitionSpec as P

MESH = pl.DeviceIdType.MESH
CHUNKS = 12
ROWS = 64
STAGES = {
    "launch": -4,
    "relay": 2,
    "reduce": 4,
    "spread": 2,
    "forward": 4,
    "share": -1,
    "combine": 0,
    "pair": 6,
    "multiply": 7,
    "finish": 9,
}
CROSSED = 2
CROSS = {"spread": -1, "cross": 7, "pair": 11, "multiply": 12}
FETCH_AT = 1
TURN_AT = 8
feature_axes = (((1,), (1,)), ((), ()))


def matmul(a, b):
    return jnp.dot(a, b, preferred_element_type=jnp.float32)


def wait_bytes(ref, sem):
    pltpu.make_async_copy(ref, ref, sem).wait()


def kernel(
    heads, weight, incoming, parked,
    act_v, total, turned_v, weight_out_v, block_v, last_weight_v,
    heads_v, weight_v, stored_v, up_v, half_v, half_in, sums, relay_in, direct_in, final_in,
    load_sem, weight_sem, send_sem, near_sem, far_sem, left_sem, right_sem, rest_sem, pair_sem,
    share_sem, relay_sem, direct_sem, final_sem, stored_sem, cross_sem,
):
    width = weight_v.shape[2]
    half = heads_v.shape[1]
    section, tensor = lax.axis_index("section"), lax.axis_index("tensor")
    z_lo, z_hi, x, core = section % 4, tensor // 8, (tensor // 2) % 4, tensor % 2
    z = z_hi * 4 + z_lo
    right, left, across = (x + 1) % 4, (x + 3) % 4, (x + 2) % 4
    above, below = (section + 1) % 16, (section + 15) % 16
    up_hi, down_hi = ((z + 1) % 8) // 4, ((z + 7) % 8) // 4

    def member(hi, column):
        return hi * 8 + column * 2 + core

    sibling = (section, tensor + 1 - 2 * core)
    to_right, to_left = (section, member(z_hi, right)), (section, member(z_hi, left))
    near_up, far_up = (above, member(up_hi, x)), (above, member(1 - up_hi, x))
    near_down, far_down = (below, member(down_hi, x)), (below, member(1 - down_hi, x))
    opposite, partner = ((section + 8) % 16, tensor), (section, (tensor + 8) % 16)

    def rows_of(hi, column):
        return pl.ds(pl.multiple_of(core * half + (hi * 4 + column) * ROWS, ROWS), ROWS)

    def own_half():
        return pl.ds(pl.multiple_of(core * half, half), half)

    def send(src, dst, stage, recv, device):
        pltpu.make_async_remote_copy(
            src_ref=src, dst_ref=dst, send_sem=send_sem.at[stage], recv_sem=recv, device_id=device, device_id_type=MESH
        ).start()

    def columns(j):
        return pl.ds(pl.multiple_of(j * width, width), width)

    def load_heads(slot, colour):
        return pltpu.make_async_copy(heads.at[:, colour], heads_v.at[slot].reshape(8, ROWS, heads_v.shape[2]), load_sem.at[slot])

    def load_weight(j):
        return pltpu.make_async_copy(weight.at[:, columns(j)], weight_v.at[j], weight_sem.at[j])

    load_heads(1, 1 - core).start()
    load_weight(0).start()
    load_heads(0, core).start()

    @pl.loop(1, CHUNKS)
    def _(j):
        load_weight(j).start()

    barrier = pltpu.get_barrier_semaphore()
    peers = (sibling, to_right, to_left, near_up, far_up, near_down, far_down, opposite, partner)
    for peer in peers:
        pl.semaphore_signal(barrier, inc=1, device_id=peer, device_id_type=MESH)

    def project(j):
        load_weight(j).wait()
        half_v[j] = matmul(heads_v[1], weight_v[j]).astype(jnp.bfloat16)

    def send_half(j):
        send(half_v.at[j], half_in.at[j], 1, share_sem.at[j], sibling)

    def share(j):
        project(j)
        send_half(j)

    def launch(j):
        own = rows_of(z_hi, x)
        send(incoming.at[:, columns(j)], up_v.at[j, own], 0, near_sem.at[j], near_down)

        @pl.when(j >= CROSSED)
        def _():
            send(incoming.at[:, columns(j)], up_v.at[j, own], 0, far_sem.at[j], far_down)

    def combine(j):
        wait_bytes(half_in.at[j], share_sem.at[j])
        both = matmul(heads_v[0], weight_v[j]) + half_in[j].astype(jnp.float32)
        sums[j] = both.astype(jnp.bfloat16).reshape(2, 4, ROWS, width)
        send(sums.at[j, 0, across], relay_in.at[j, 0], 2, relay_sem.at[j, 0], to_right)
        send(sums.at[j, 1, across], relay_in.at[j, 1], 2, relay_sem.at[j, 1], to_left)
        send(sums.at[j, 1, right], direct_in.at[j, 0, 1], 2, direct_sem.at[j], to_right)
        send(sums.at[j, 0, left], direct_in.at[j, 1, 0], 2, direct_sem.at[j], to_left)

    def relay(j):
        for hi, column, device in ((0, right, to_right), (1, left, to_left)):
            wait_bytes(relay_in.at[j, hi], relay_sem.at[j, hi])
            added = sums[j, hi, column].astype(jnp.float32) + relay_in[j, hi].astype(jnp.float32)
            sums[j, hi, column] = added.astype(jnp.bfloat16)
            send(sums.at[j, hi, column], direct_in.at[j, hi, hi], 3, direct_sem.at[j], device)

    def reduce(j):
        wait_bytes(direct_in.at[j], direct_sem.at[j])
        for hi in range(2):
            added = sums[j, hi, x].astype(jnp.float32) + direct_in[j, 0, hi].astype(jnp.float32)
            sums[j, hi, x] = (added + direct_in[j, 1, hi].astype(jnp.float32)).astype(jnp.bfloat16)
        send(sums.at[j, 1 - up_hi, x], final_in.at[j, 1], 4, final_sem.at[j], far_up)
        send(sums.at[j, up_hi, x], final_in.at[j, 0], 4, final_sem.at[j], near_up)

    def finish(j):
        wait_bytes(final_in.at[j], final_sem.at[j])
        act_v[j] = (final_in[j, 0].astype(jnp.float32) + final_in[j, 1].astype(jnp.float32)).astype(jnp.bfloat16)

    def spread(j):
        near, far = up_v.at[j, rows_of(up_hi, x)], up_v.at[j, rows_of(1 - up_hi, x)]
        wait_bytes(near, near_sem.at[j])
        send(near, near, 5, left_sem.at[j], to_right)

        @pl.when(j < CROSSED)
        def _():
            send(near, near, 5, rest_sem.at[j], to_left)

        @pl.when(j >= CROSSED)
        def _():
            wait_bytes(far, far_sem.at[j])
            send(far, far, 5, right_sem.at[j], to_left)

    def forward(j):
        near, far = up_v.at[j, rows_of(up_hi, x)], up_v.at[j, rows_of(1 - up_hi, x)]

        @pl.when(j >= CROSSED)
        def _():
            send(near, near, 5, rest_sem.at[j], to_left)
            send(far, far, 5, rest_sem.at[j], to_right)

        passed_near, passed_far = up_v.at[j, rows_of(up_hi, left)], up_v.at[j, rows_of(1 - up_hi, right)]
        wait_bytes(passed_near, left_sem.at[j])
        send(passed_near, passed_near, 6, rest_sem.at[j], to_right)

        @pl.when(j >= CROSSED)
        def _():
            wait_bytes(passed_far, right_sem.at[j])
            send(passed_far, passed_far, 6, rest_sem.at[j], to_left)

    def cross(j):
        wait_bytes(up_v.at[j, pl.ds(0, 2 * ROWS)], rest_sem.at[j])
        mine = up_v.at[j, pl.ds(pl.multiple_of(core * half + up_hi * 4 * ROWS, 4 * ROWS), 4 * ROWS)]
        send(mine, mine, 9, cross_sem.at[j], partner)

    def pair(j):
        @pl.when(j >= CROSSED)
        def _():
            wait_bytes(up_v.at[j, pl.ds(0, 4 * ROWS)], rest_sem.at[j])

        @pl.when(j < CROSSED)
        def _():
            wait_bytes(up_v.at[j, pl.ds(0, 4 * ROWS)], cross_sem.at[j])

        mine = up_v.at[j, own_half()]
        send(mine, mine, 7, pair_sem.at[j], sibling)

    def fetch_stored(block):
        for colour in range(2):
            send(parked.at[block, colour], stored_v.at[colour, block], 8, stored_sem, opposite)

    def turn():
        wait_bytes(stored_v, stored_sem)
        turned_v[...] = stored_v[...].reshape(2 * half, stored_v.shape[3]).T

    def multiply(j):
        wait_bytes(up_v.at[j, pl.ds(0, half)], pair_sem.at[j])
        block = up_v[j]
        term = lax.dot_general(block, weight_v[j], feature_axes, preferred_element_type=jnp.float32)

        total[...] += term
        weight_out_v[j] = matmul(turned_v[...], block).astype(jnp.bfloat16)

    stages = dict(
        launch=launch, share=share, combine=combine, relay=relay, reduce=reduce, spread=spread, forward=forward, pair=pair,
        multiply=multiply, finish=finish, cross=cross,
    )

    load_heads(1, 1 - core).wait()
    project(0)
    pl.semaphore_wait(barrier, len(peers))
    send_half(0)
    pl.loop(0, -STAGES["launch"])(launch)
    total[...] = jnp.zeros_like(total)
    load_heads(0, core).wait()
    for j in range(-CROSS["spread"]):
        spread(j)

    @pl.loop(0, CHUNKS + max(STAGES.values()))
    def _(i):
        pl.when((i >= FETCH_AT) & (i < FETCH_AT + 8))(lambda: fetch_stored(i - FETCH_AT))
        pl.when(i == TURN_AT)(turn)
        for name, start in STAGES.items():
            first = CROSSED if name in CROSS else max(-start, 0)
            count = CHUNKS - 1 if name == "multiply" else CHUNKS
            pl.when((i >= start + first) & (i < start + count))(functools.partial(stages[name], i - start))
        for name, start in CROSS.items():
            pl.when((i >= max(start, 0)) & (i < start + CROSSED))(functools.partial(stages[name], i - start))

    wait_bytes(up_v.at[CHUNKS - 1, pl.ds(0, half)], pair_sem.at[CHUNKS - 1])
    block_v[...] = up_v[CHUNKS - 1]
    last_weight_v[...] = weight_v[CHUNKS - 1]
    blocks = half_v.reshape(CHUNKS * 8, ROWS, width)
    sent = {
        0: 2 * CHUNKS - CROSSED,
        1: 8 * CHUNKS,
        2: 4 * CHUNKS,
        3: 2 * CHUNKS,
        4: 2 * CHUNKS,
        5: 4 * CHUNKS - 2 * CROSSED,
        6: 2 * CHUNKS - CROSSED,
        7: 8 * CHUNKS,
        9: 4 * CROSSED,
    }
    for stage, count in sent.items():
        wait_bytes(blocks.at[pl.ds(0, count)], send_sem.at[stage])
    wait_bytes(stored_v, send_sem.at[8])


def publish(
    act_v, total, turned_v, weight_out_v, block_v, last_weight_v,
    activation, heads_gradient, weight_gradient,
    heads_out_v, last_v, sem,
):
    width = act_v.shape[2]

    def columns(j):
        return pl.ds(j * width, width)

    for j in range(CHUNKS - 1):
        pltpu.make_async_copy(weight_out_v.at[j], weight_gradient.at[:, columns(j)], sem.at[0]).start()
    for j in range(CHUNKS):
        pltpu.make_async_copy(act_v.at[j], activation.at[:, columns(j)], sem.at[1]).start()
    block = block_v[...]
    term = lax.dot_general(block, last_weight_v[...], feature_axes, preferred_element_type=jnp.float32)
    heads_out_v[...] = (total[...] + term).astype(jnp.bfloat16).reshape(heads_out_v.shape)
    for colour in range(2):
        pltpu.make_async_copy(heads_out_v.at[colour], heads_gradient.at[:, colour], sem.at[2]).start()
    last_v[...] = matmul(turned_v[...], block).astype(jnp.bfloat16)
    pltpu.make_async_copy(last_v, weight_gradient.at[:, columns(CHUNKS - 1)], sem.at[3]).start()
    wait_bytes(weight_out_v, sem.at[0])
    wait_bytes(act_v, sem.at[1])
    wait_bytes(heads_out_v, sem.at[2])
    wait_bytes(last_v, sem.at[3])


def section_step(heads_out, projection, incoming, parked):
    weight = projection[0]
    depth, model = weight.shape
    tokens = heads_out.shape[1]
    half, width = tokens // 2, model // CHUNKS
    blocked = (8, 2, ROWS, depth)
    bf16, f32 = jnp.bfloat16, jnp.float32
    dma = pltpu.SemaphoreType.DMA
    per_chunk = dma((CHUNKS,))
    outs = pl.pallas_call(
        kernel,
        out_shape=(
            pltpu.VMEM((CHUNKS, ROWS, width), bf16),
            pltpu.VMEM((tokens, depth), f32),
            pltpu.VMEM((depth, tokens), bf16),
            pltpu.VMEM((CHUNKS - 1, depth, width), bf16),
            pltpu.VMEM((tokens, width), bf16),
            pltpu.VMEM((depth, width), bf16),
        ),
        in_specs=[pl.BlockSpec(memory_space=pl.ANY)] * 4,
        out_specs=[pl.BlockSpec(memory_space=pltpu.VMEM)] * 6,
        scratch_shapes=[
            pltpu.VMEM((2, half, depth), bf16),
            pltpu.VMEM((CHUNKS, depth, width), bf16),
            pltpu.VMEM((2, 8, ROWS, depth), bf16),
            pltpu.VMEM((CHUNKS, tokens, width), bf16),
            pltpu.VMEM((CHUNKS, half, width), bf16),
            pltpu.VMEM((CHUNKS, half, width), bf16),
            pltpu.VMEM((CHUNKS, 2, 4, ROWS, width), bf16),
            pltpu.VMEM((CHUNKS, 2, ROWS, width), bf16),
            pltpu.VMEM((CHUNKS, 2, 2, ROWS, width), bf16),
            pltpu.VMEM((CHUNKS, 2, ROWS, width), bf16),
            dma((2,)),
            per_chunk,
            dma((10,)),
            per_chunk,
            per_chunk,
            per_chunk,
            per_chunk,
            per_chunk,
            per_chunk,
            per_chunk,
            dma((CHUNKS, 2)),
            per_chunk,
            per_chunk,
            dma,
            per_chunk,
        ],
        compiler_params=pltpu.CompilerParams(collective_id=0, has_side_effects=True, vmem_limit_bytes=50 << 20),
        cost_estimate=pl.CostEstimate(flops=6 * tokens * depth * model, bytes_accessed=14 << 20, transcendentals=0),
        name="relay_section",
    )(heads_out.reshape(blocked), weight, incoming[0], parked.reshape(blocked))
    activation, heads_gradient, weight_gradient = pl.pallas_call(
        publish,
        out_shape=(
            jax.ShapeDtypeStruct((ROWS, model), bf16),
            jax.ShapeDtypeStruct(blocked, bf16),
            jax.ShapeDtypeStruct((depth, model), bf16),
        ),
        in_specs=[pl.BlockSpec(memory_space=pltpu.VMEM)] * 6,
        out_specs=[pl.BlockSpec(memory_space=pl.ANY)] * 3,
        scratch_shapes=[pltpu.VMEM((2, 8, ROWS, depth), bf16), pltpu.VMEM((depth, width), bf16), dma((4,))],
        compiler_params=pltpu.CompilerParams(vmem_limit_bytes=12 << 20),
        name="publish",
    )(*(pltpu.with_memory_space_constraint(out, pltpu.VMEM) for out in outs))
    return activation[None], heads_gradient.reshape(1, tokens, depth), weight_gradient[None]


def solution(mesh):
    whole_tokens = P("section", None, "tensor")
    rows = P("section", "tensor", None)
    return jax.shard_map(
        section_step,
        mesh=mesh,
        in_specs=(whole_tokens, rows, rows, whole_tokens),
        out_specs=(rows, whole_tokens, rows),
        check_vma=False,
    )
```
